32 devices in a mesh: kv: 8 (over y, x, core), tp: 4 (over z).
Axes of the slice: x: 2, y: 2, z: 4, core: 2. Of those that a mesh axis runs over, the one named last changes fastest.
Arguments:
- queries: bfloat16 [2, 6, 16384], P(None, None, 'tp'), may hold values from -12 to 12
- new_kv: bfloat16 [2, 2, 6, 1024], P(None, None, None, 'tp'), may hold values from -9 to 9
- kv_cache: bfloat16 [2, 256, 256, 1024], P(None, 'kv', None, 'tp'), may hold values from -6 to 6
- kv_scales: float32 [2, 256, 8], P(None, 'kv', 'tp'), may hold values from 0.5 to 1.5
- context_lens: int32 [6], replicated, may hold values from 1 to 24320
- block_owner: int32 [256], P('kv'), may hold values from 0 to 6, as said below
- block_index: int32 [256], P('kv'), may hold values from 0 to 94, as said below
- out_weight: bfloat16 [8, 2048, 16384], P('tp', 'kv'), may hold values from -0.046875 to 0.046875
Outputs:
- layer_out: bfloat16 [2, 6, 16384], P(None, None, ('kv', 'tp'))
The draws below stay inside these ranges and needn't reach their ends.
Inputs may be any that keep to these rules, and one draw needn't show every extreme that they name: `block_owner`: each slot names the request whose block it holds, or 6 for an empty slot. Every block 0 to ceil(context_lens[r] / 256) - 1 of every request is held by exactly one slot. In each group of 32 consecutive slots the used ones come first, and some group uses all of them. `block_index`: an empty slot holds 0.
All inputs are finite; a program needn't handle non-finite values.
Results may differ from the reference program's by a relative error of at most 0.0051.
Values sent between devices are 32-bit elements; how exact they have to be, the bound alone decides.
A program may use at most 192 MiB of HBM per device.

```python
import math
import jax
import jax.numpy as jnp
from jax import lax

D = 16384
HQ = 128
KVH = 8
HD = 128
R = 6
STEPS = 2
BLOCK = 256
BLK_DEV = 32
SLOTS = 256
G = 16
N_KV = 8


def layout_plan(key):
    key_full, key_rank, key_order, key_trim = jax.random.split(key, 4)
    lower = max(1, BLK_DEV // 4)
    filled_count = N_KV // 2 * BLK_DEV + (N_KV - N_KV // 2) * lower
    small_count = max(1, filled_count // (2 * R))
    big_count = filled_count - (R - 1) * small_count
    device_rank = jax.random.permutation(key_full, N_KV)
    used = jnp.where(device_rank < N_KV // 2, BLK_DEV, lower).astype(jnp.int32)
    request_rank = jax.random.permutation(key_rank, R)
    counts = jnp.where(request_rank == 0, big_count, small_count).astype(jnp.int32)
    starts = jnp.cumsum(counts) - counts
    slot_ids = jnp.arange(SLOTS, dtype=jnp.int32)
    order_keys = jax.random.randint(key_order, (SLOTS,), 0, 65536) * SLOTS + slot_ids
    order_keys = jnp.where(slot_ids < filled_count, order_keys, order_keys + 2 ** 30)
    ordering = jnp.argsort(order_keys, stable=True).astype(jnp.int32)
    in_use = (jnp.arange(BLK_DEV)[None, :] < used[:, None]).reshape(-1)
    ranking = jnp.maximum(jnp.cumsum(in_use.astype(jnp.int32)) - 1, 0)
    global_block = ordering[ranking]
    owner_rows = (global_block[:, None] >= starts[None, 1:]).astype(jnp.int32).sum(1)
    picked = (jnp.arange(R)[None, :] == owner_rows[:, None]).astype(jnp.int32)
    offsets = global_block - (picked * starts[None, :]).sum(1)
    owners = jnp.where(in_use, owner_rows, R).astype(jnp.int32)
    numbers = jnp.where(in_use, offsets, 0).astype(jnp.int32)
    trims = jnp.where(request_rank == 0, 0, jax.random.randint(key_trim, (R,), 0, BLOCK))
    lengths = (counts * BLOCK - trims).astype(jnp.int32)
    return (owners, numbers, lengths)


def draw_block_owner(key, part):
    return layout_plan(key)[0]


def draw_block_index(key, part):
    return layout_plan(key)[1]


def draw_context_lens(key, part):
    return layout_plan(key)[2]


def draw_queries(key, part):
    key = jax.random.fold_in(key, 11)
    heads_per = HQ // KVH
    base = 1.5 * jax.random.truncated_normal(key, -4.0, 4.0, (STEPS, R, KVH, heads_per, HD), jnp.float32)
    return base.reshape(STEPS, R, HQ * HD).astype(jnp.bfloat16)


def draw_kv_cache(key, part):
    key = jax.random.fold_in(key, 12)
    base = jax.random.truncated_normal(key, -6.0, 6.0, (2, SLOTS, BLOCK, KVH, HD), jnp.float32)
    return base.reshape(2, SLOTS, BLOCK, KVH * HD).astype(jnp.bfloat16)


def shard_levels(rng, extent, cuts, low, high):
    factor_of, own = 1.0, jax.random.fold_in(rng, 6)
    for position, blocks in cuts:
        heights = jnp.exp(jax.random.uniform(jax.random.fold_in(own, position), (blocks,), jnp.float32, low / len(cuts), high / len(cuts)))
        factor_of = factor_of * jnp.repeat(heights, extent[position] // blocks).reshape([-1 if axis == position else 1 for axis in range(len(extent))])
    return factor_of


def centred(rng, shape, deviation, bound, shards=(), kind=jnp.bfloat16):
    values = jax.random.normal(rng, shape, jnp.float32) * deviation
    if len(shards) > 0:
        values = shard_levels(rng, shape, shards, -0.22, 0.18) * values
    return jnp.clip(values, min=-bound, max=bound).astype(kind)


def setup_inputs(seed: int = 0) -> dict:
    arg_keys = jax.random.split(jax.random.key(seed), 9)
    queries = draw_queries(jax.random.fold_in(arg_keys[8], 71), 0)
    new_kv = centred(arg_keys[1], (2, STEPS, R, KVH * HD), 1.5, 9.0, ((3, 4),))
    kv_cache = draw_kv_cache(jax.random.fold_in(arg_keys[8], 71), 0)
    kv_scales = jnp.clip(jnp.exp(math.log(1.5) - 1.0986123 * jax.random.uniform(arg_keys[3], (2, SLOTS, KVH), jnp.float32) ** shard_levels(arg_keys[3], (2, SLOTS, KVH), ((1, 8), (2, 4)), -0.2, 0.2)), 0.5, 1.5)
    context_lens = draw_context_lens(jax.random.fold_in(arg_keys[8], 71), 0)
    block_owner = draw_block_owner(jax.random.fold_in(arg_keys[8], 71), 0)
    block_index = draw_block_index(jax.random.fold_in(arg_keys[8], 71), 0)
    out_weight = centred(arg_keys[7], (KVH, G * HD, D), (HQ * HD) ** -0.5, 0.046875, ((0, 4), (1, 8)))
    return {"queries": queries, "new_kv": new_kv, "kv_cache": kv_cache, "kv_scales": kv_scales, "context_lens": context_lens, "block_owner": block_owner, "block_index": block_index, "out_weight": out_weight}


very_negative = -1e+30

def group_partials(queries, cache, scales, context_lens, block_owner, block_index):
    heads_per = HQ // KVH
    query = queries.reshape(STEPS, R, KVH, heads_per, HD).transpose(1, 2, 3, 0, 4).reshape(R, KVH, heads_per * STEPS, HD)
    slot_count = cache.shape[1]
    key_rows = cache[0].reshape(slot_count, BLOCK, KVH, HD).astype(jnp.float32)
    value_rows = cache[1].reshape(slot_count, BLOCK, KVH, HD).astype(jnp.float32)
    safe_owner = jnp.minimum(block_owner, R - 1).astype(jnp.int32)
    chosen = jnp.take(query, safe_owner, axis=0).astype(jnp.float32)
    factor = 1.0 / math.sqrt(HD)
    scores = jnp.einsum('bksd,btkd->bkst', chosen, key_rows) * (scales[0][:, :, None, None] * factor)
    positions = block_index[:, None] * BLOCK + jnp.arange(BLOCK, dtype=jnp.int32)[None, :]
    length_cap = jnp.take(context_lens, safe_owner)
    usable = (block_owner < R)[:, None] & (positions < length_cap[:, None])
    masked = jnp.where(usable[:, None, None, :], scores, very_negative)
    block_peak = masked.max(-1)
    member = block_owner[None, :] == jnp.arange(R, dtype=jnp.int32)[:, None]
    peak = jnp.where(member[:, :, None, None], block_peak[None], very_negative).max(1)
    slot_peak = jnp.take(peak, safe_owner, axis=0)
    softened = jnp.where(usable[:, None, None, :], jnp.exp(masked - slot_peak[..., None]), 0.0)
    slot_total = softened.sum(-1)
    rounded = lax.optimization_barrier(softened.astype(jnp.bfloat16)).astype(jnp.float32)
    mixed_values = jnp.einsum('bkst,btkd->bksd', rounded, value_rows) * scales[1][:, :, None, None]
    weights = member.astype(jnp.float32)
    total = jnp.einsum('rb,bks->rks', weights, slot_total, precision=lax.Precision.HIGHEST)
    numer = jnp.einsum('rb,bksd->rksd', weights, mixed_values, precision=lax.Precision.HIGHEST)
    return (peak, total, numer)

def finish(peak, total, numer, query, new_keys, new_values):
    factor = 1.0 / math.sqrt(HD)
    fresh_scores = jnp.einsum('rkgsd,trkd->rkgst', query.astype(jnp.float32), new_keys.astype(jnp.float32)) * factor
    causal = jnp.arange(STEPS)[None, :] <= jnp.arange(STEPS)[:, None]
    causal_scores = jnp.where(causal, fresh_scores, very_negative)
    peak_all = jnp.maximum(peak, causal_scores.max(-1))
    retain = jnp.exp(peak - peak_all)
    fresh = jnp.where(causal, jnp.exp(fresh_scores - peak_all[..., None]), 0.0)
    denominator = total * retain + fresh.sum(-1)
    numerator = numer * retain[..., None] + jnp.einsum('rkgst,trkd->rkgsd', fresh, new_values.astype(jnp.float32), precision=lax.Precision.HIGHEST)
    return (numerator / denominator[..., None]).astype(jnp.bfloat16)

def reference(queries, new_kv, kv_cache, kv_scales, context_lens, block_owner, block_index, out_weight):
    heads_per = HQ // KVH

    def one_group(shard_id):
        start = (shard_id * BLK_DEV).astype(jnp.int32)
        cache = lax.dynamic_slice_in_dim(kv_cache, start, BLK_DEV, 1)
        scales = lax.dynamic_slice_in_dim(kv_scales, start, BLK_DEV, 1)
        owners = lax.dynamic_slice_in_dim(block_owner, start, BLK_DEV, 0)
        numbers = lax.dynamic_slice_in_dim(block_index, start, BLK_DEV, 0)
        return group_partials(queries, cache, scales, context_lens, owners, numbers)
    peaks, totals, numers = lax.map(one_group, jnp.arange(N_KV, dtype=jnp.int32))
    peak = peaks.max(0)
    weight = jnp.exp(peaks - peak[None])
    total = (weight * totals).sum(0)
    numer = (weight[..., None] * numers).sum(0)
    peak = peak.reshape(R, KVH, heads_per, STEPS)
    total = total.reshape(R, KVH, heads_per, STEPS)
    numer = numer.reshape(R, KVH, heads_per, STEPS, HD)
    query = queries.reshape(STEPS, R, KVH, heads_per, HD).transpose(1, 2, 3, 0, 4)
    newer = new_kv.reshape(2, STEPS, R, KVH, HD)
    attended = finish(peak, total, numer, query, newer[0], newer[1])
    flat = attended.transpose(3, 0, 1, 2, 4).reshape(STEPS * R, HQ * HD)
    result = jnp.dot(flat, out_weight.reshape(HQ * HD, D), preferred_element_type=jnp.float32)
    return result.astype(jnp.bfloat16).reshape(STEPS, R, D)
```

```python
import functools
import math

import jax
import jax.numpy as jnp
from jax import lax
from jax.experimental import pallas as pl
from jax.experimental.pallas import tpu as pltpu
from jax.sharding import PartitionSpec as P

HQ = 128
KVH = 8
HD = 128
R = 6
STEPS = 2
BLOCK = 256

very_negative = -1e30
MESH = pl.DeviceIdType.MESH


class Sizes:
    def __init__(self, n_kv, n_tp, kv_heads, slots, width):
        self.n_kv, self.n_tp, self.kv_heads, self.slots = n_kv, n_tp, kv_heads, slots
        self.share = HQ // KVH // n_kv
        self.used_rows = kv_heads * self.share * STEPS
        self.rows = -(-self.used_rows // 8) * 8
        self.all_rows = n_kv * self.rows
        self.depth = kv_heads * HD
        self.stack = R * self.rows
        self.message = self.stack + 8
        self.cols = width // (n_kv * n_tp)
        self.packed = self.cols % 256 == 0
        self.half = self.cols // 2 if self.packed else self.cols
        self.piece = 3 * self.half if self.packed else 2 * self.half
        self.chunk = width // n_kv
        self.pairs = n_kv // 2
        self.load_parts = 4 if slots % 4 == 0 else 1


def flip(index, distance):
    result, bit = index, 1
    while bit <= distance:
        if distance & bit:
            result = result + bit * (1 - 2 * ((index // bit) % 2))
        bit *= 2
    return result


def row_head(z, shape):
    row = lax.broadcasted_iota(jnp.int32, shape, 0) % z.rows
    return row // (z.share * STEPS)


def by_head(z, head, pieces):
    result = pieces[-1]
    for k in range(z.kv_heads - 2, -1, -1):
        result = jnp.where(head == k, pieces[k], result)
    return result


def attend(
    z, lens, owner, number, scales, q_ref, cache, msg, kv_buf, qb, s_buf, m_buf, t_buf, n_buf, peak_buf, sems
):
    part = z.slots // z.load_parts

    def load(which, n):
        piece = pl.ds(n * part, part)
        return pltpu.make_async_copy(cache.at[which, piece], kv_buf.at[which, piece], sems.at[which, n])

    for which in range(2):
        for n in range(z.load_parts):
            load(which, n).start()

    head = row_head(z, (z.all_rows, HD))
    lane = lax.broadcasted_iota(jnp.int32, (z.all_rows, BLOCK), 1)
    factor = 1.0 / math.sqrt(HD)
    for r in range(R):
        rows = q_ref[r].reshape(z.all_rows, HD)
        for k in range(z.kv_heads):
            qb[r, :, k * HD : (k + 1) * HD] = jnp.where(head == k, rows, 0.0).astype(jnp.bfloat16)

    def cap_of(b):
        own = owner[b]
        safe = jnp.minimum(own, R - 1)
        return safe, jnp.where(own < R, lens[safe], 0) - number[b] * BLOCK

    def score(b):
        safe, cap = cap_of(b)
        product = lax.dot_general(
            qb[safe], kv_buf[0, b], (((1,), (1,)), ((), ())), preferred_element_type=jnp.float32
        )
        scale = by_head(
            z, head, [jnp.full((z.all_rows, HD), scales[0, b, k] * factor) for k in range(z.kv_heads)]
        )
        scale = jnp.concatenate([scale] * (BLOCK // HD), 1)
        masked = jnp.where(lane < cap, product * scale, very_negative)
        s_buf[b] = masked
        m_buf[b] = jnp.maximum(masked[:, :HD], masked[:, HD:])

    def mix(b):
        safe, cap = cap_of(b)
        top = peak_buf[safe]
        top = jnp.concatenate([top] * (BLOCK // HD), 1)
        weight = jnp.where(lane < cap, jnp.exp(s_buf[b] - top), 0.0)
        t_buf[b] = weight[:, :HD] + weight[:, HD:]
        product = jnp.dot(weight.astype(jnp.bfloat16), kv_buf[1, b], preferred_element_type=jnp.float32)
        n_buf[b] = by_head(
            z, head, [product[:, k * HD : (k + 1) * HD] * scales[1, b, k] for k in range(z.kv_heads)]
        )

    def sweep(which, step):
        def group(n, carry):
            load(which, n).wait()
            for i in range(part):
                step(n * part + i)
            return carry

        lax.fori_loop(0, z.load_parts, group, 0)

    sweep(0, score)

    def peak_of(r):
        def step(b, top):
            return jnp.maximum(top, m_buf[b] + jnp.where(owner[b] == r, 0.0, 2 * very_negative))

        start = jnp.full((z.all_rows, HD), very_negative, jnp.float32)
        top = lax.fori_loop(0, z.slots, step, start, unroll=8)
        return jnp.broadcast_to(top.max(1, keepdims=True), top.shape)

    for r in range(R):
        peak_buf[r] = peak_of(r)
    sweep(1, mix)

    row = lax.broadcasted_iota(jnp.int32, (z.all_rows, HD), 0) % z.rows
    column = lax.broadcasted_iota(jnp.int32, (z.all_rows, HD), 1)
    peaks = jnp.zeros((z.all_rows, HD), jnp.float32)
    totals = jnp.zeros((z.all_rows, HD), jnp.float32)
    for r in range(R):

        def step(b, sums):
            keep = jnp.where(owner[b] == r, 1.0, 0.0)
            return sums[0] + keep * t_buf[b], sums[1] + keep * n_buf[b]

        zero = jnp.zeros((z.all_rows, HD), jnp.float32)
        total, numer = lax.fori_loop(0, z.slots, step, (zero, zero), unroll=8)
        here = column == r * z.rows + row
        peaks = peaks + jnp.where(here, peak_buf[r], 0.0)
        totals = totals + jnp.where(here, total.sum(1, keepdims=True), 0.0)
        msg[:, r * z.rows : (r + 1) * z.rows, :] = numer.reshape(z.n_kv, z.rows, HD)
    msg[:, z.stack :, :] = jnp.zeros((z.n_kv, 8, HD), jnp.float32)
    msg[:, z.stack : z.stack + 1, :] = peaks.reshape(z.n_kv, z.rows, HD).sum(1, keepdims=True)
    msg[:, z.stack + 1 : z.stack + 2, :] = totals.reshape(z.n_kv, z.rows, HD).sum(1, keepdims=True)


def project(
    z, q_ref, new_ref, w_ref, msg, out_ref,
    w_buf, got, new_x, att, a_rows, sent1, sent2, got1, got2, sums, got3, whole,
    w_sem, m_send, m_recv, send1, recv1, send2, recv2, send3, recv3,
):
    kv, tp = lax.axis_index("kv"), lax.axis_index("tp")
    high, side = kv // 2, kv % 2
    partner = kv + 1 - 2 * side
    order = list(range(z.pairs - 1, -1, -1))

    barrier = pltpu.get_barrier_semaphore()
    for d in range(1, z.n_kv):
        pl.semaphore_signal(barrier, inc=1, device_id=(flip(kv, d), tp), device_id_type=MESH)
    for e in range(1, z.n_tp):
        pl.semaphore_signal(barrier, inc=1, device_id=(kv, (tp + e) % z.n_tp), device_id_type=MESH)

    owners = [2 * flip(high, d) + 1 - side for d in order] + [2 * flip(high, d) + side for d in order]

    def load(n):
        start = pl.multiple_of(owners[n] * z.chunk, z.chunk)
        return pltpu.make_async_copy(w_ref.at[:, :, pl.ds(start, z.chunk)], w_buf.at[n], w_sem.at[n])

    for n in range(z.n_kv):
        load(n).start()

    pl.semaphore_wait(barrier, z.n_kv - 1 + z.n_tp - 1)

    def remote(src, dst, send, recv, target):
        return pltpu.make_async_remote_copy(
            src_ref=src, dst_ref=dst, send_sem=send, recv_sem=recv, device_id=target, device_id_type=MESH
        )

    exchange = []
    for d in range(z.n_kv - 1, 0, -1):
        there = flip(kv, d)
        copy = remote(msg.at[there], got.at[d - 1], m_send.at[d - 1], m_recv.at[d - 1], (there, tp))
        copy.start()
        exchange.append(copy)

    factor = 1.0 / math.sqrt(HD)
    newer = new_ref[...].astype(jnp.float32)
    small = row_head(z, (z.rows, HD))
    for a in range(2):
        for u in range(STEPS):
            for r in range(R):
                pieces = [
                    jnp.broadcast_to(newer[a, u, r : r + 1, k * HD : (k + 1) * HD], (z.rows, HD))
                    for k in range(z.kv_heads)
                ]
                new_x[a, u, r * z.rows : (r + 1) * z.rows, :] = by_head(z, small, pieces)
    query = q_ref[:, kv].reshape(z.stack, HD)
    step_of = lax.broadcasted_iota(jnp.int32, (z.stack, 1), 0) % STEPS
    fresh = [(query * new_x[0, u]).sum(1, keepdims=True) * factor for u in range(STEPS)]
    fresh = [jnp.where(u <= step_of, fresh[u], very_negative) for u in range(STEPS)]
    fresh_top = functools.reduce(jnp.maximum, fresh)
    a_rows[...] = jnp.zeros_like(a_rows)

    for copy in exchange:
        copy.wait()
    spot = lax.broadcasted_iota(jnp.int32, (z.stack, HD), 0) == lax.broadcasted_iota(
        jnp.int32, (z.stack, HD), 1
    )

    def expand(values):
        return jnp.where(spot, values, 0.0).sum(1, keepdims=True)

    stats = [msg[kv, z.stack :, :]] + [got[d, z.stack :, :] for d in range(z.n_kv - 1)]
    peak = functools.reduce(jnp.maximum, [s[0:1] for s in stats])
    weights = [jnp.exp(s[0:1] - peak) for s in stats]
    total = functools.reduce(jnp.add, [w * s[1:2] for w, s in zip(weights, stats)])
    numer = expand(weights[0]) * msg[kv, : z.stack, :]
    for d in range(z.n_kv - 1):
        numer = numer + expand(weights[d + 1]) * got[d, : z.stack, :]
    peak, total = expand(peak), expand(total)
    top = jnp.maximum(peak, fresh_top)
    retain = jnp.exp(peak - top)
    fresh = [jnp.where(u <= step_of, jnp.exp(fresh[u] - top), 0.0) for u in range(STEPS)]
    numer, total = numer * retain, total * retain
    for u in range(STEPS):
        numer = numer + fresh[u] * new_x[1, u]
        total = total + fresh[u]
    att[...] = numer / total

    count = STEPS * R
    for c in range(z.kv_heads * z.share):
        for s in range(STEPS):
            a_rows[0, s * R : (s + 1) * R, c * HD : (c + 1) * HD] = att[
                pl.ds(c * STEPS + s, R, stride=z.rows), :
            ]
    a_rows[1, 0:8, :] = a_rows[0, 0:8, :]
    a_rows[1, 12 : 12 + count - 8, :] = a_rows[0, 8:count, :]
    low = a_rows[0].astype(jnp.bfloat16)
    late = a_rows[1].astype(jnp.bfloat16)
    inner = z.share * HD

    def product(rows, n, start):
        parts = [
            jnp.dot(
                rows[:, k * inner : (k + 1) * inner],
                w_buf[n, k, :, start : start + z.half],
                preferred_element_type=jnp.float32,
            )
            for k in range(z.kv_heads)
        ]
        return functools.reduce(jnp.add, parts)

    def fill(n, t, put):
        first = product(low, n, t * z.cols)
        if z.packed:
            second = product(late, n, t * z.cols + z.half)
            put(slice(0, z.half), first[0:8])
            put(slice(z.half, 2 * z.half), second[0:8])
            put(slice(2 * z.half, 3 * z.half), first[8:16] + second[8:16])
        else:
            put(slice(0, z.half), first[0:8])
            put(slice(z.half, 2 * z.half), first[8:16])

    paired = []
    for n in range(z.pairs):
        load(n).wait()
        for t in range(z.n_tp):

            def put(where, value):
                sent1[n, t, :, where] = value

            fill(n, t, put)
        copy = remote(sent1.at[n], got1.at[n], send1.at[n], recv1.at[n], (partner, tp))
        copy.start()
        paired.append(copy)

    spread = []
    for n, d in enumerate(order):
        load(z.pairs + n).wait()
        paired[n].wait_recv()
        for t in range(z.n_tp):

            def put(where, value):
                sent2[n, t, :, where] = value + got1[n, t, :, where]

            fill(z.pairs + n, t, put)
        if d > 0:
            there = 2 * flip(high, d) + side
            copy = remote(sent2.at[n], got2.at[d - 1], send2.at[d - 1], recv2.at[d - 1], (there, tp))
            copy.start()
            spread.append(copy)

    for copy in spread:
        copy.wait_recv()
    last = []

    def add_up(t):
        value = sent2[z.pairs - 1, t]
        for d in range(z.pairs - 1):
            value = value + got2[d, t]
        return value

    for e in range(1, z.n_tp):
        there = (tp + e) % z.n_tp
        sums[e - 1] = add_up(there)
        copy = remote(sums.at[e - 1], got3.at[e - 1], send3.at[e - 1], recv3.at[e - 1], (kv, there))
        copy.start()
        last.append(copy)
    value = add_up(tp)
    for copy in last:
        copy.wait_recv()
    for e in range(z.n_tp - 1):
        value = value + got3[e]
    if z.packed:
        whole[0:8, : z.half] = value[:, : z.half]
        whole[0:8, z.half :] = value[:, z.half : 2 * z.half]
        whole[8:12, : z.half] = value[0:4, 2 * z.half :]
        whole[8:12, z.half :] = value[4:8, 2 * z.half :]
    else:
        whole[0:8, :] = value[:, : z.half]
        whole[8:16, :] = value[:, z.half :]
    for s in range(STEPS):
        out_ref[s] = whole[s * R : (s + 1) * R, :]
    for copy in paired + spread + last:
        copy.wait_send()


def attend_scratch(z):
    f32, bf16 = jnp.float32, jnp.bfloat16
    tile = (z.slots, z.all_rows, HD)
    return [
        pltpu.VMEM((2, z.slots, BLOCK, z.depth), bf16),
        pltpu.VMEM((R, z.all_rows, z.depth), bf16),
        pltpu.VMEM((z.slots, z.all_rows, BLOCK), f32),
        pltpu.VMEM(tile, f32),
        pltpu.VMEM(tile, f32),
        pltpu.VMEM(tile, f32),
        pltpu.VMEM((R, z.all_rows, HD), f32),
        pltpu.SemaphoreType.DMA((2, z.load_parts)),
    ]


def project_scratch(z):
    f32, bf16 = jnp.float32, jnp.bfloat16
    dma = pltpu.SemaphoreType.DMA
    rest, others = max(z.pairs - 1, 1), max(z.n_tp - 1, 1)
    part = (z.n_tp, 8, z.piece)
    return [
        pltpu.VMEM((z.n_kv, z.kv_heads, z.share * HD, z.chunk), bf16),
        pltpu.VMEM((z.n_kv - 1, z.message, HD), f32),
        pltpu.VMEM((2, STEPS, z.stack, HD), f32),
        pltpu.VMEM((z.stack, HD), f32),
        pltpu.VMEM((2, 16, z.kv_heads * z.share * HD), f32),
        pltpu.VMEM((z.pairs, *part), f32),
        pltpu.VMEM((z.pairs, *part), f32),
        pltpu.VMEM((z.pairs, *part), f32),
        pltpu.VMEM((rest, *part), f32),
        pltpu.VMEM((others, 8, z.piece), f32),
        pltpu.VMEM((others, 8, z.piece), f32),
        pltpu.VMEM((16, z.cols), f32),
        dma((z.n_kv,)),
        dma((z.n_kv - 1,)),
        dma((z.n_kv - 1,)),
        dma((z.pairs,)),
        dma((z.pairs,)),
        dma((rest,)),
        dma((rest,)),
        dma((others,)),
        dma((others,)),
    ]


def spaces(*names):
    kinds = {"s": pltpu.SMEM, "v": pltpu.VMEM, "h": pl.ANY}
    return [pl.BlockSpec(memory_space=kinds[name]) for name in names]


def shards(
    queries, new_kv, kv_cache, kv_scales, context_lens, block_owner, block_index, out_weight
):
    n_kv, n_tp = lax.axis_size("kv"), lax.axis_size("tp")
    kv_heads = kv_cache.shape[3] // HD
    z = Sizes(n_kv, n_tp, kv_heads, kv_cache.shape[1], out_weight.shape[2])
    query = (
        queries.reshape(STEPS, R, kv_heads, n_kv, z.share, HD)
        .transpose(1, 3, 2, 4, 0, 5)
        .reshape(R, n_kv, z.used_rows, HD)
        .astype(jnp.float32)
    )
    query = jnp.pad(query, ((0, 0), (0, 0), (0, z.rows - z.used_rows), (0, 0)))
    msg = pl.pallas_call(
        functools.partial(attend, z),
        out_shape=jax.ShapeDtypeStruct((n_kv, z.message, HD), jnp.float32),
        in_specs=spaces(*"ssssvh"),
        out_specs=spaces("v")[0],
        scratch_shapes=attend_scratch(z),
        compiler_params=pltpu.CompilerParams(vmem_limit_bytes=56 * 2**20),
        name="attend",
    )(context_lens, block_owner, block_index, kv_scales, query, kv_cache)
    out = pl.pallas_call(
        functools.partial(project, z),
        out_shape=jax.ShapeDtypeStruct((STEPS, R, z.cols), jnp.float32),
        in_specs=spaces(*"vvhv"),
        out_specs=spaces("v")[0],
        scratch_shapes=project_scratch(z),
        compiler_params=pltpu.CompilerParams(
            vmem_limit_bytes=56 * 2**20, collective_id=0, has_side_effects=True
        ),
        name="project",
    )(query, new_kv, out_weight, msg)
    return out.astype(jnp.bfloat16)


def solution(mesh):
    placed = (
        P(None, None, "tp"),
        P(None, None, None, "tp"),
        P(None, "kv", None, "tp"),
        P(None, "kv", "tp"),
        P(),
        P("kv"),
        P("kv"),
        P("tp", "kv", None),
    )
    return jax.shard_map(
        shards, mesh=mesh, in_specs=placed, out_specs=P(None, None, ("kv", "tp")), check_vma=False
    )
```

```python
import functools
import math

import jax
import jax.numpy as jnp
from jax import lax
from jax.experimental import pallas as pl
from jax.experimental.pallas import tpu as pltpu
from jax.sharding import PartitionSpec as P

HQ = 128
KVH = 8
HD = 128
R = 6
STEPS = 2
BLOCK = 256

very_negative = -1e30
MESH = pl.DeviceIdType.MESH


class Sizes:
    def __init__(self, n_kv, n_tp, kv_heads, slots, width):
        self.n_kv, self.n_tp, self.kv_heads, self.slots = n_kv, n_tp, kv_heads, slots
        self.share = HQ // KVH // n_kv
        self.used_rows = kv_heads * self.share * STEPS
        self.rows = -(-self.used_rows // 8) * 8
        self.all_rows = n_kv * self.rows
        self.depth = kv_heads * HD
        self.stack = R * self.rows
        self.message = self.stack + 8
        self.cols = width // (n_kv * n_tp)
        self.packed = self.cols % 256 == 0
        self.half = self.cols // 2 if self.packed else self.cols
        self.piece = 3 * self.half if self.packed else 2 * self.half
        self.width = width
        self.inner = self.share * HD
        self.pairs = n_kv // 2
        self.load_parts = 4 if slots % 4 == 0 else 1


def flip(index, distance):
    result, bit = index, 1
    while bit <= distance:
        if distance & bit:
            result = result + bit * (1 - 2 * ((index // bit) % 2))
        bit *= 2
    return result


def row_head(z, shape):
    row = lax.broadcasted_iota(jnp.int32, shape, 0) % z.rows
    return row // (z.share * STEPS)


def by_head(z, head, pieces):
    result = pieces[-1]
    for k in range(z.kv_heads - 2, -1, -1):
        result = jnp.where(head == k, pieces[k], result)
    return result


def attend(
    z, lens, owner, number, scales, queries, msg, q_rows, kv_buf, qb, s_buf, m_buf, t_buf, n_buf, peak_buf, load, between
):
    part = z.slots // z.load_parts
    head = row_head(z, (z.all_rows, HD))
    lane = lax.broadcasted_iota(jnp.int32, (z.all_rows, BLOCK), 1)
    factor = 1.0 / math.sqrt(HD)
    if z.used_rows < z.rows:
        q_rows[...] = jnp.zeros_like(q_rows)
    for r in range(R):
        flat = queries[r].astype(jnp.float32)
        for k in range(z.kv_heads):
            for j in range(z.n_kv):
                for g in range(z.share):
                    h = (k * z.n_kv + j) * z.share + g
                    row = (k * z.share + g) * STEPS
                    q_rows[r, j, row : row + STEPS, :] = flat[:, h * HD : (h + 1) * HD]
    for r in range(R):
        rows = q_rows[r].reshape(z.all_rows, HD)
        for k in range(z.kv_heads):
            qb[r, :, k * HD : (k + 1) * HD] = jnp.where(head == k, rows, 0.0).astype(jnp.bfloat16)
    blank = jnp.zeros((z.all_rows, HD), jnp.float32)
    m_buf[z.slots] = blank + very_negative
    t_buf[z.slots] = blank
    n_buf[z.slots] = blank

    def cap_of(b):
        own = owner[b]
        safe = jnp.minimum(own, R - 1)
        return safe, jnp.where(own < R, lens[safe], 0) - number[b] * BLOCK

    def score(b, before):
        safe, cap = cap_of(b)
        product = lax.dot_general(
            qb[safe], kv_buf[0, b], (((1,), (1,)), ((), ())), preferred_element_type=jnp.float32
        )
        scale = by_head(z, head, [jnp.full((z.all_rows, HD), scales[0, k, b] * factor) for k in range(z.kv_heads)])
        scale = jnp.concatenate([scale] * (BLOCK // HD), 1)
        masked = jnp.where(lane < cap, product * scale, very_negative)
        s_buf[b] = masked
        m_buf[b] = jnp.maximum(jnp.maximum(masked[:, :HD], masked[:, HD:]), m_buf[before])

    def mix(b, before):
        safe, cap = cap_of(b)
        top = peak_buf[safe]
        top = jnp.concatenate([top] * (BLOCK // HD), 1)
        weight = jnp.where(lane < cap, jnp.exp(s_buf[b] - top), 0.0)
        t_buf[b] = weight[:, :HD] + weight[:, HD:] + t_buf[before]
        product = jnp.dot(weight.astype(jnp.bfloat16), kv_buf[1, b], preferred_element_type=jnp.float32)
        mixed = by_head(z, head, [product[:, k * HD : (k + 1) * HD] * scales[1, k, b] for k in range(z.kv_heads)])
        n_buf[b] = mixed + n_buf[before]

    def sweep(which, step):
        def group(n, last):
            load(which, n).wait()
            last = list(last)
            for i in range(part):
                b = n * part + i
                own = owner[b]
                before = jnp.int32(z.slots)
                for r in range(R):
                    before = jnp.where(own == r, last[r], before)
                step(b, before)
                last = [jnp.where(own == r, b, last[r]) for r in range(R)]
            return tuple(last)

        return lax.fori_loop(0, z.load_parts, group, (jnp.int32(z.slots),) * R)

    last = sweep(0, score)
    between()
    for r in range(R):
        peak_buf[r] = jnp.broadcast_to(m_buf[last[r]].max(1, keepdims=True), (z.all_rows, HD))
    last = sweep(1, mix)

    row = lax.broadcasted_iota(jnp.int32, (z.all_rows, HD), 0) % z.rows
    column = lax.broadcasted_iota(jnp.int32, (z.all_rows, HD), 1)
    peaks, totals = blank, blank
    for r in range(R):
        here = column == r * z.rows + row
        peaks = peaks + jnp.where(here, peak_buf[r], 0.0)
        totals = totals + jnp.where(here, t_buf[last[r]].sum(1, keepdims=True), 0.0)
        msg[:, r * z.rows : (r + 1) * z.rows, :] = n_buf[last[r]].reshape(z.n_kv, z.rows, HD)
    msg[:, z.stack :, :] = jnp.zeros((z.n_kv, 8, HD), jnp.float32)
    msg[:, z.stack : z.stack + 1, :] = peaks.reshape(z.n_kv, z.rows, HD).sum(1, keepdims=True)
    msg[:, z.stack + 1 : z.stack + 2, :] = totals.reshape(z.n_kv, z.rows, HD).sum(1, keepdims=True)


def layer(
    z, lens, owner, number, scales, queries, new_ref, cache, w_ref, out_ref,
    kv_buf, q_rows, qb, s_buf, m_buf, t_buf, n_buf, peak_buf, msg,
    w_buf, got, new_x, att, a_rows, sent1, got1, sent2, got2, sums, got3, whole,
    c_sem, w_sem, m_send, m_recv, send1, recv1, send2, recv2, send3, recv3,
):
    kv, tp = lax.axis_index("kv"), lax.axis_index("tp")
    high, side = kv // 2, kv % 2
    partner = kv + 1 - 2 * side
    order = list(range(z.pairs - 1, -1, -1))
    turns = [(e + 1) % z.n_tp for e in range(z.n_tp)]
    part = z.slots // z.load_parts

    def load(which, n):
        piece = pl.ds(n * part, part)
        return pltpu.make_async_copy(cache.at[which, piece], kv_buf.at[which, piece], c_sem.at[which, n])

    for which in range(2):
        for n in range(z.load_parts):
            load(which, n).start()

    barrier = pltpu.get_barrier_semaphore()
    for d in range(1, z.n_kv):
        pl.semaphore_signal(barrier, inc=1, device_id=(flip(kv, d), tp), device_id_type=MESH)
    for e in range(1, z.n_tp):
        pl.semaphore_signal(barrier, inc=1, device_id=(kv, (tp + e) % z.n_tp), device_id_type=MESH)

    block = z.inner // 4

    def load_weight(k, n):
        piece = pl.ds(n * block, block)
        return pltpu.make_async_copy(w_ref.at[k, piece], w_buf.at[k, piece], w_sem.at[k, n])

    def load_weights():
        for k in range(z.kv_heads):
            for n in range(4):
                load_weight(k, n).start()

    attend(
        z, lens, owner, number, scales, queries, msg, q_rows, kv_buf, qb, s_buf, m_buf, t_buf, n_buf, peak_buf, load, load_weights
    )
    pl.semaphore_wait(barrier, z.n_kv - 1 + z.n_tp - 1)

    def remote(src, dst, send, recv, target):
        return pltpu.make_async_remote_copy(
            src_ref=src, dst_ref=dst, send_sem=send, recv_sem=recv, device_id=target, device_id_type=MESH
        )

    exchange = []
    for d in range(z.n_kv - 1, 0, -1):
        there = flip(kv, d)
        copy = remote(msg.at[there], got.at[d - 1], m_send.at[d - 1], m_recv.at[d - 1], (there, tp))
        copy.start()
        exchange.append(copy)

    factor = 1.0 / math.sqrt(HD)
    newer = new_ref[...].astype(jnp.float32)
    small = row_head(z, (z.rows, HD))
    for a in range(2):
        for u in range(STEPS):
            for r in range(R):
                pieces = [
                    jnp.broadcast_to(newer[a, r, u : u + 1, k * HD : (k + 1) * HD], (z.rows, HD))
                    for k in range(z.kv_heads)
                ]
                new_x[a, u, r * z.rows : (r + 1) * z.rows, :] = by_head(z, small, pieces)
    query = q_rows[:, kv].reshape(z.stack, HD)
    step_of = lax.broadcasted_iota(jnp.int32, (z.stack, 1), 0) % STEPS
    fresh = [(query * new_x[0, u]).sum(1, keepdims=True) * factor for u in range(STEPS)]
    fresh = [jnp.where(u <= step_of, fresh[u], very_negative) for u in range(STEPS)]
    fresh_top = functools.reduce(jnp.maximum, fresh)
    a_rows[...] = jnp.zeros_like(a_rows)

    for copy in exchange:
        copy.wait_recv()
    spot = lax.broadcasted_iota(jnp.int32, (z.stack, HD), 0) == lax.broadcasted_iota(
        jnp.int32, (z.stack, HD), 1
    )

    def expand(values):
        return jnp.where(spot, values, 0.0).sum(1, keepdims=True)

    stats = [msg[kv, z.stack :, :]] + [got[d, z.stack :, :] for d in range(z.n_kv - 1)]
    peak = functools.reduce(jnp.maximum, [s[0:1] for s in stats])
    weights = [jnp.exp(s[0:1] - peak) for s in stats]
    total = functools.reduce(jnp.add, [w * s[1:2] for w, s in zip(weights, stats)])
    numer = expand(weights[0]) * msg[kv, : z.stack, :]
    for d in range(z.n_kv - 1):
        numer = numer + expand(weights[d + 1]) * got[d, : z.stack, :]
    peak, total = expand(peak), expand(total)
    top = jnp.maximum(peak, fresh_top)
    retain = jnp.exp(peak - top)
    fresh = [jnp.where(u <= step_of, jnp.exp(fresh[u] - top), 0.0) for u in range(STEPS)]
    numer, total = numer * retain, total * retain
    for u in range(STEPS):
        numer = numer + fresh[u] * new_x[1, u]
        total = total + fresh[u]
    att[...] = numer / total

    count = STEPS * R
    for c in range(z.kv_heads * z.share):
        for s in range(STEPS):
            a_rows[0, s * R : (s + 1) * R, c * HD : (c + 1) * HD] = att[
                pl.ds(c * STEPS + s, R, stride=z.rows), :
            ]
    a_rows[1, 0:8, :] = a_rows[0, 0:8, :]
    a_rows[1, 12 : 12 + count - 8, :] = a_rows[0, 8:count, :]
    low = a_rows[0].astype(jnp.bfloat16)
    late = a_rows[1].astype(jnp.bfloat16)

    for k in range(z.kv_heads):
        for n in range(4):
            load_weight(k, n).wait()

    def product(rows, start):
        columns = pl.ds(pl.multiple_of(start, z.half), z.half)
        parts = [
            jnp.dot(
                rows[:, k * z.inner : (k + 1) * z.inner],
                w_buf[k, :, columns],
                preferred_element_type=jnp.float32,
            )
            for k in range(z.kv_heads)
        ]
        return functools.reduce(jnp.add, parts)

    def fill(j, t, put):
        start = (j * z.n_tp + t) * z.cols
        first = product(low, start)
        if z.packed:
            second = product(late, start + z.half)
            put(slice(0, z.half), first[0:8])
            put(slice(z.half, 2 * z.half), second[0:8])
            put(slice(2 * z.half, 3 * z.half), first[8:16] + second[8:16])
        else:
            put(slice(0, z.half), first[0:8])
            put(slice(z.half, 2 * z.half), first[8:16])

    paired = []
    for i, e in enumerate(turns):
        for n, d in enumerate(order):

            def put(where, value):
                sent1[i, n, :, where] = value

            fill(2 * flip(high, d) + 1 - side, (tp + e) % z.n_tp, put)
        copy = remote(sent1.at[i], got1.at[i], send1.at[i], recv1.at[i], (partner, tp))
        copy.start()
        paired.append(copy)

    spread = []
    for i, e in enumerate(turns):
        paired[i].wait_recv()
        arriving = []
        for n, d in enumerate(order):

            def put(where, value):
                sent2[i, n, :, where] = value + got1[i, n, :, where]

            there = 2 * flip(high, d) + side
            fill(there, (tp + e) % z.n_tp, put)
            if d > 0:
                copy = remote(
                    sent2.at[i, n], got2.at[i, d - 1], send2.at[i, d - 1], recv2.at[i, d - 1], (there, tp)
                )
                copy.start()
                arriving.append(copy)
        spread.append(arriving)

    last = []
    for i, e in enumerate(turns):
        for copy in spread[i]:
            copy.wait_recv()
        value = sent2[i, z.pairs - 1]
        for d in range(z.pairs - 1):
            value = value + got2[i, d]
        if e > 0:
            sums[e - 1] = value
            there = (tp + e) % z.n_tp
            copy = remote(sums.at[e - 1], got3.at[e - 1], send3.at[e - 1], recv3.at[e - 1], (kv, there))
            copy.start()
            last.append(copy)
    for copy in last:
        copy.wait_recv()
    for e in range(z.n_tp - 1):
        value = value + got3[e]
    if z.packed:
        whole[0:8, : z.half] = value[:, : z.half]
        whole[0:8, z.half :] = value[:, z.half : 2 * z.half]
        whole[8:12, : z.half] = value[0:4, 2 * z.half :]
        whole[8:12, z.half :] = value[4:8, 2 * z.half :]
    else:
        whole[0:8, :] = value[:, : z.half]
        whole[8:16, :] = value[:, z.half :]
    for r in range(R):
        for s in range(STEPS):
            out_ref[r, s : s + 1, :] = whole[s * R + r : s * R + r + 1, :]
    for copy in exchange:
        copy.wait_send()
    for copy in paired + sum(spread, []) + last:
        copy.wait_send()


def scratch(z):
    f32, bf16 = jnp.float32, jnp.bfloat16
    dma = pltpu.SemaphoreType.DMA
    tile = (z.slots + 1, z.all_rows, HD)
    rest, others = max(z.pairs - 1, 1), max(z.n_tp - 1, 1)
    part = (8, z.piece)
    return [
        pltpu.VMEM((2, z.slots, BLOCK, z.depth), bf16),
        pltpu.VMEM((R, z.n_kv, z.rows, HD), f32),
        pltpu.VMEM((R, z.all_rows, z.depth), bf16),
        pltpu.VMEM((z.slots, z.all_rows, BLOCK), f32),
        pltpu.VMEM(tile, f32),
        pltpu.VMEM(tile, f32),
        pltpu.VMEM(tile, f32),
        pltpu.VMEM((R, z.all_rows, HD), f32),
        pltpu.VMEM((z.n_kv, z.message, HD), f32),
        pltpu.VMEM((z.kv_heads, z.inner, z.width), bf16),
        pltpu.VMEM((z.n_kv - 1, z.message, HD), f32),
        pltpu.VMEM((2, STEPS, z.stack, HD), f32),
        pltpu.VMEM((z.stack, HD), f32),
        pltpu.VMEM((2, 16, z.kv_heads * z.inner), f32),
        pltpu.VMEM((z.n_tp, z.pairs, *part), f32),
        pltpu.VMEM((z.n_tp, z.pairs, *part), f32),
        pltpu.VMEM((z.n_tp, z.pairs, *part), f32),
        pltpu.VMEM((z.n_tp, rest, *part), f32),
        pltpu.VMEM((others, *part), f32),
        pltpu.VMEM((others, *part), f32),
        pltpu.VMEM((16, z.cols), f32),
        dma((2, z.load_parts)),
        dma((z.kv_heads, 4)),
        dma((z.n_kv - 1,)),
        dma((z.n_kv - 1,)),
        dma((z.n_tp,)),
        dma((z.n_tp,)),
        dma((z.n_tp, rest)),
        dma((z.n_tp, rest)),
        dma((others,)),
        dma((others,)),
    ]


def spaces(*names):
    kinds = {"s": pltpu.SMEM, "v": pltpu.VMEM, "h": pl.ANY}
    return [pl.BlockSpec(memory_space=kinds[name]) for name in names]


def shards(
    queries, new_kv, kv_cache, kv_scales, context_lens, block_owner, block_index, out_weight
):
    n_kv, n_tp = lax.axis_size("kv"), lax.axis_size("tp")
    kv_heads = kv_cache.shape[3] // HD
    z = Sizes(n_kv, n_tp, kv_heads, kv_cache.shape[1], out_weight.shape[2])
    out = pl.pallas_call(
        functools.partial(layer, z),
        out_shape=jax.ShapeDtypeStruct((R, STEPS, z.cols), jnp.float32),
        in_specs=spaces(*"ssssvvhh"),
        out_specs=spaces("v")[0],
        scratch_shapes=scratch(z),
        compiler_params=pltpu.CompilerParams(
            vmem_limit_bytes=56 * 2**20, collective_id=0, has_side_effects=True
        ),
        name="layer",
    )(
        context_lens,
        block_owner,
        block_index,
        kv_scales.transpose(0, 2, 1),
        queries.transpose(1, 0, 2),
        new_kv.transpose(0, 2, 1, 3),
        kv_cache,
        out_weight,
    )
    return out.transpose(1, 0, 2).astype(jnp.bfloat16)


def solution(mesh):
    placed = (
        P(None, None, "tp"),
        P(None, None, None, "tp"),
        P(None, "kv", None, "tp"),
        P(None, "kv", "tp"),
        P(),
        P("kv"),
        P("kv"),
        P("tp", "kv", None),
    )
    return jax.shard_map(
        shards, mesh=mesh, in_specs=placed, out_specs=P(None, None, ("kv", "tp")), check_vma=False
    )
```

```python
import functools
import math

import jax
import jax.numpy as jnp
from jax import lax
from jax.experimental import pallas as pl
from jax.experimental.pallas import tpu as pltpu
from jax.sharding import PartitionSpec as P

HQ = 128
KVH = 8
HD = 128
R = 6
STEPS = 2
BLOCK = 256

very_negative = -1e30
MESH = pl.DeviceIdType.MESH


class Sizes:
    def __init__(self, n_kv, n_tp, kv_heads, slots, width):
        self.n_kv, self.n_tp, self.kv_heads, self.slots = n_kv, n_tp, kv_heads, slots
        self.share = HQ // KVH // n_kv
        self.used_rows = kv_heads * self.share * STEPS
        self.rows = -(-self.used_rows // 8) * 8
        self.all_rows = n_kv * self.rows
        self.depth = kv_heads * HD
        self.stack = R * self.rows
        self.message = self.stack + 8
        self.cols = width // (n_kv * n_tp)
        self.packed = self.cols % 256 == 0
        self.half = self.cols // 2 if self.packed else self.cols
        self.piece = 3 * self.half if self.packed else 2 * self.half
        self.width = width
        self.inner = self.share * HD
        self.pairs = n_kv // 2
        self.groups = [1] * n_tp
        self.load_parts = 4 if slots % 4 == 0 else 1


def flip(index, distance):
    result, bit = index, 1
    while bit <= distance:
        if distance & bit:
            result = result + bit * (1 - 2 * ((index // bit) % 2))
        bit *= 2
    return result


def row_head(z, shape):
    row = lax.broadcasted_iota(jnp.int32, shape, 0) % z.rows
    return row // (z.share * STEPS)


def by_head(z, head, pieces):
    result = pieces[-1]
    for k in range(z.kv_heads - 2, -1, -1):
        result = jnp.where(head == k, pieces[k], result)
    return result


def attend(
    z, lens, owner, number, scales, queries, msg, q_rows, kv_buf, qb, s_buf, m_buf, t_buf, n_buf, peak_buf, load, between, newest
):
    part = z.slots // z.load_parts
    head = row_head(z, (z.all_rows, HD))
    lane = lax.broadcasted_iota(jnp.int32, (z.all_rows, BLOCK), 1)
    factor = 1.0 / math.sqrt(HD)
    if z.used_rows < z.rows:
        q_rows[...] = jnp.zeros_like(q_rows)
    for r in range(R):
        flat = queries[r].astype(jnp.float32)
        for k in range(z.kv_heads):
            for j in range(z.n_kv):
                for g in range(z.share):
                    h = (k * z.n_kv + j) * z.share + g
                    row = (k * z.share + g) * STEPS
                    q_rows[r, j, row : row + STEPS, :] = flat[:, h * HD : (h + 1) * HD]
    for r in range(R):
        rows = q_rows[r].reshape(z.all_rows, HD)
        for k in range(z.kv_heads):
            qb[r, :, k * HD : (k + 1) * HD] = jnp.where(head == k, rows, 0.0).astype(jnp.bfloat16)
    blank = jnp.zeros((z.all_rows, HD), jnp.float32)
    m_buf[z.slots] = blank + very_negative
    t_buf[z.slots] = blank
    n_buf[z.slots] = blank

    def cap_of(b):
        own = owner[b]
        safe = jnp.minimum(own, R - 1)
        return safe, jnp.where(own < R, lens[safe], 0) - number[b] * BLOCK

    def score(b, before):
        safe, cap = cap_of(b)
        product = lax.dot_general(
            qb[safe], kv_buf[0, b], (((1,), (1,)), ((), ())), preferred_element_type=jnp.float32
        )
        scale = by_head(z, head, [jnp.full((z.all_rows, HD), scales[0, k, b] * factor) for k in range(z.kv_heads)])
        scale = jnp.concatenate([scale] * (BLOCK // HD), 1)
        masked = jnp.where(lane < cap, product * scale, very_negative)
        s_buf[b] = masked
        m_buf[b] = jnp.maximum(jnp.maximum(masked[:, :HD], masked[:, HD:]), m_buf[before])

    def mix(b, before):
        safe, cap = cap_of(b)
        top = peak_buf[safe]
        top = jnp.concatenate([top] * (BLOCK // HD), 1)
        weight = jnp.where(lane < cap, jnp.exp(s_buf[b] - top), 0.0)
        t_buf[b] = weight[:, :HD] + weight[:, HD:] + t_buf[before]
        product = jnp.dot(weight.astype(jnp.bfloat16), kv_buf[1, b], preferred_element_type=jnp.float32)
        mixed = by_head(z, head, [product[:, k * HD : (k + 1) * HD] * scales[1, k, b] for k in range(z.kv_heads)])
        n_buf[b] = mixed + n_buf[before]

    def sweep(which, step):
        def group(n, last):
            load(which, n).wait()
            last = list(last)
            for i in range(part):
                b = n * part + i
                own = owner[b]
                before = jnp.int32(z.slots)
                for r in range(R):
                    before = jnp.where(own == r, last[r], before)
                step(b, before)
                last = [jnp.where(own == r, b, last[r]) for r in range(R)]
            return tuple(last)

        return lax.fori_loop(0, z.load_parts, group, (jnp.int32(z.slots),) * R)

    fresh = newest()
    last = sweep(0, score)
    between()
    for r in range(R):
        peak_buf[r] = jnp.broadcast_to(m_buf[last[r]].max(1, keepdims=True), (z.all_rows, HD))
    last = sweep(1, mix)

    row = lax.broadcasted_iota(jnp.int32, (z.all_rows, HD), 0) % z.rows
    column = lax.broadcasted_iota(jnp.int32, (z.all_rows, HD), 1)
    peaks, totals = blank, blank
    for r in range(R):
        here = column == r * z.rows + row
        peaks = peaks + jnp.where(here, peak_buf[r], 0.0)
        totals = totals + jnp.where(here, t_buf[last[r]].sum(1, keepdims=True), 0.0)
        msg[:, r * z.rows : (r + 1) * z.rows, :] = n_buf[last[r]].reshape(z.n_kv, z.rows, HD)
    msg[:, z.stack :, :] = jnp.zeros((z.n_kv, 8, HD), jnp.float32)
    msg[:, z.stack : z.stack + 1, :] = peaks.reshape(z.n_kv, z.rows, HD).sum(1, keepdims=True)
    msg[:, z.stack + 1 : z.stack + 2, :] = totals.reshape(z.n_kv, z.rows, HD).sum(1, keepdims=True)
    return fresh


def layer(
    z, lens, owner, number, scales, queries, new_ref, cache, w_ref, out_ref,
    kv_buf, q_rows, qb, s_buf, m_buf, t_buf, n_buf, peak_buf, msg,
    w_buf, got, new_x, att, a_rows, sent1, got1, sent2, got2, sums, got3, whole,
    c_sem, w_sem, m_send, m_recv, send1, recv1, send2, recv2, send3, recv3,
):
    kv, tp = lax.axis_index("kv"), lax.axis_index("tp")
    high, side = kv // 2, kv % 2
    partner = kv + 1 - 2 * side
    order = list(range(z.pairs - 1, -1, -1))
    turns = [(e + 1) % z.n_tp for e in range(z.n_tp)]
    part = z.slots // z.load_parts

    def load(which, n):
        piece = pl.ds(n * part, part)
        return pltpu.make_async_copy(cache.at[which, piece], kv_buf.at[which, piece], c_sem.at[which, n])

    for which in range(2):
        for n in range(z.load_parts):
            load(which, n).start()

    barrier = pltpu.get_barrier_semaphore()
    for d in range(1, z.n_kv):
        pl.semaphore_signal(barrier, inc=1, device_id=(flip(kv, d), tp), device_id_type=MESH)
    for e in range(1, z.n_tp):
        pl.semaphore_signal(barrier, inc=1, device_id=(kv, (tp + e) % z.n_tp), device_id_type=MESH)

    block = z.inner // 4

    def load_weight(k, n):
        piece = pl.ds(n * block, block)
        return pltpu.make_async_copy(w_ref.at[k, piece], w_buf.at[k, piece], w_sem.at[k, n])

    def load_weights():
        for k in range(z.kv_heads):
            for n in range(4):
                load_weight(k, n).start()

    def newest():
        factor = 1.0 / math.sqrt(HD)
        newer = new_ref[...].astype(jnp.float32)
        small = row_head(z, (z.rows, HD))
        for a in range(2):
            for u in range(STEPS):
                for r in range(R):
                    pieces = [
                        jnp.broadcast_to(newer[a, r, u : u + 1, k * HD : (k + 1) * HD], (z.rows, HD))
                        for k in range(z.kv_heads)
                    ]
                    new_x[a, u, r * z.rows : (r + 1) * z.rows, :] = by_head(z, small, pieces)
        query = q_rows[:, kv].reshape(z.stack, HD)
        step_of = lax.broadcasted_iota(jnp.int32, (z.stack, 1), 0) % STEPS
        fresh = [(query * new_x[0, u]).sum(1, keepdims=True) * factor for u in range(STEPS)]
        fresh = [jnp.where(u <= step_of, fresh[u], very_negative) for u in range(STEPS)]
        fresh_top = functools.reduce(jnp.maximum, fresh)
        a_rows[...] = jnp.zeros_like(a_rows)
        return fresh, fresh_top, step_of

    fresh, fresh_top, step_of = attend(
        z, lens, owner, number, scales, queries, msg, q_rows, kv_buf, qb, s_buf, m_buf, t_buf, n_buf, peak_buf, load, load_weights, newest
    )
    pl.semaphore_wait(barrier, z.n_kv - 1 + z.n_tp - 1)

    def remote(src, dst, send, recv, target):
        return pltpu.make_async_remote_copy(
            src_ref=src, dst_ref=dst, send_sem=send, recv_sem=recv, device_id=target, device_id_type=MESH
        )

    exchange = []
    for d in range(z.n_kv - 1, 0, -1):
        there = flip(kv, d)
        copy = remote(msg.at[there], got.at[d - 1], m_send.at[d - 1], m_recv.at[d - 1], (there, tp))
        copy.start()
        exchange.append(copy)

    for copy in exchange:
        copy.wait_recv()
    spot = lax.broadcasted_iota(jnp.int32, (z.stack, HD), 0) == lax.broadcasted_iota(
        jnp.int32, (z.stack, HD), 1
    )

    def expand(values):
        return jnp.where(spot, values, 0.0).sum(1, keepdims=True)

    stats = [msg[kv, z.stack :, :]] + [got[d, z.stack :, :] for d in range(z.n_kv - 1)]
    peak = functools.reduce(jnp.maximum, [s[0:1] for s in stats])
    weights = [jnp.exp(s[0:1] - peak) for s in stats]
    total = functools.reduce(jnp.add, [w * s[1:2] for w, s in zip(weights, stats)])
    numer = expand(weights[0]) * msg[kv, : z.stack, :]
    for d in range(z.n_kv - 1):
        numer = numer + expand(weights[d + 1]) * got[d, : z.stack, :]
    peak, total = expand(peak), expand(total)
    top = jnp.maximum(peak, fresh_top)
    retain = jnp.exp(peak - top)
    fresh = [jnp.where(u <= step_of, jnp.exp(fresh[u] - top), 0.0) for u in range(STEPS)]
    numer, total = numer * retain, total * retain
    for u in range(STEPS):
        numer = numer + fresh[u] * new_x[1, u]
        total = total + fresh[u]
    att[...] = numer / total

    count = STEPS * R
    for c in range(z.kv_heads * z.share):
        for s in range(STEPS):
            a_rows[0, s * R : (s + 1) * R, c * HD : (c + 1) * HD] = att[
                pl.ds(c * STEPS + s, R, stride=z.rows), :
            ]
    a_rows[1, 0:8, :] = a_rows[0, 0:8, :]
    a_rows[1, 12 : 12 + count - 8, :] = a_rows[0, 8:count, :]
    low = a_rows[0].astype(jnp.bfloat16)
    late = a_rows[1].astype(jnp.bfloat16)

    for k in range(z.kv_heads):
        for n in range(4):
            load_weight(k, n).wait()

    def product(rows, start):
        columns = pl.ds(pl.multiple_of(start, z.half), z.half)
        parts = [
            jnp.dot(
                rows[:, k * z.inner : (k + 1) * z.inner],
                w_buf[k, :, columns],
                preferred_element_type=jnp.float32,
            )
            for k in range(z.kv_heads)
        ]
        return functools.reduce(jnp.add, parts)

    def fill(j, t, put):
        start = (j * z.n_tp + t) * z.cols
        first = product(low, start)
        if z.packed:
            second = product(late, start + z.half)
            put(slice(0, z.half), first[0:8])
            put(slice(z.half, 2 * z.half), second[0:8])
            put(slice(2 * z.half, 3 * z.half), first[8:16] + second[8:16])
        else:
            put(slice(0, z.half), first[0:8])
            put(slice(z.half, 2 * z.half), first[8:16])

    paired, spread, last, totals = [], [], [], []
    groups = z.groups
    firsts = [sum(groups[:i]) for i in range(len(groups))]

    def pair_step(i):
        for m in range(firsts[i], firsts[i] + groups[i]):
            for n, d in enumerate(order):

                def put(where, value):
                    sent1[m, n, :, where] = value

                fill(2 * flip(high, d) + 1 - side, (tp + turns[m]) % z.n_tp, put)
        piece = pl.ds(firsts[i], groups[i])
        copy = remote(sent1.at[piece], got1.at[piece], send1.at[i], recv1.at[i], (partner, tp))
        copy.start()
        paired.append(copy)

    def spread_step(i):
        paired[i].wait_recv()
        piece = pl.ds(firsts[i], groups[i])
        arriving = []
        for n, d in enumerate(order):
            there = 2 * flip(high, d) + side
            for m in range(firsts[i], firsts[i] + groups[i]):

                def put(where, value):
                    sent2[n, m, :, where] = value + got1[m, n, :, where]

                fill(there, (tp + turns[m]) % z.n_tp, put)
            if d > 0:
                copy = remote(
                    sent2.at[n, piece], got2.at[d - 1, piece], send2.at[i, d - 1], recv2.at[i, d - 1], (there, tp)
                )
                copy.start()
                arriving.append(copy)
        spread.append(arriving)

    def last_step(i):
        for copy in spread[i]:
            copy.wait_recv()
        for m in range(firsts[i], firsts[i] + groups[i]):
            e = turns[m]
            value = sent2[z.pairs - 1, m]
            for d in range(z.pairs - 1):
                value = value + got2[d, m]
            totals.append(value)
            if e > 0:
                sums[e - 1] = value
                there = (tp + e) % z.n_tp
                copy = remote(sums.at[e - 1], got3.at[e - 1], send3.at[e - 1], recv3.at[e - 1], (kv, there))
                copy.start()
                last.append(copy)

    ahead, lag = 2, 2
    for i in range(min(ahead, len(groups))):
        pair_step(i)
    for i in range(len(groups)):
        spread_step(i)
        if i + ahead < len(groups):
            pair_step(i + ahead)
        if i >= lag:
            last_step(i - lag)
    for i in range(max(len(groups) - lag, 0), len(groups)):
        last_step(i)
    value = totals[-1]
    for copy in last:
        copy.wait_recv()
    for e in range(z.n_tp - 1):
        value = value + got3[e]
    if z.packed:
        whole[0:8, : z.half] = value[:, : z.half]
        whole[0:8, z.half :] = value[:, z.half : 2 * z.half]
        whole[8:12, : z.half] = value[0:4, 2 * z.half :]
        whole[8:12, z.half :] = value[4:8, 2 * z.half :]
    else:
        whole[0:8, :] = value[:, : z.half]
        whole[8:16, :] = value[:, z.half :]
    for r in range(R):
        for s in range(STEPS):
            out_ref[r, s : s + 1, :] = whole[s * R + r : s * R + r + 1, :]
    for copy in exchange:
        copy.wait_send()
    for copy in paired + sum(spread, []) + last:
        copy.wait_send()


def scratch(z):
    f32, bf16 = jnp.float32, jnp.bfloat16
    dma = pltpu.SemaphoreType.DMA
    tile = (z.slots + 1, z.all_rows, HD)
    rest, others = max(z.pairs - 1, 1), max(z.n_tp - 1, 1)
    part = (8, z.piece)
    return [
        pltpu.VMEM((2, z.slots, BLOCK, z.depth), bf16),
        pltpu.VMEM((R, z.n_kv, z.rows, HD), f32),
        pltpu.VMEM((R, z.all_rows, z.depth), bf16),
        pltpu.VMEM((z.slots, z.all_rows, BLOCK), f32),
        pltpu.VMEM(tile, f32),
        pltpu.VMEM(tile, f32),
        pltpu.VMEM(tile, f32),
        pltpu.VMEM((R, z.all_rows, HD), f32),
        pltpu.VMEM((z.n_kv, z.message, HD), f32),
        pltpu.VMEM((z.kv_heads, z.inner, z.width), bf16),
        pltpu.VMEM((z.n_kv - 1, z.message, HD), f32),
        pltpu.VMEM((2, STEPS, z.stack, HD), f32),
        pltpu.VMEM((z.stack, HD), f32),
        pltpu.VMEM((2, 16, z.kv_heads * z.inner), f32),
        pltpu.VMEM((z.n_tp, z.pairs, *part), f32),
        pltpu.VMEM((z.n_tp, z.pairs, *part), f32),
        pltpu.VMEM((z.pairs, z.n_tp, *part), f32),
        pltpu.VMEM((rest, z.n_tp, *part), f32),
        pltpu.VMEM((others, *part), f32),
        pltpu.VMEM((others, *part), f32),
        pltpu.VMEM((16, z.cols), f32),
        dma((2, z.load_parts)),
        dma((z.kv_heads, 4)),
        dma((z.n_kv - 1,)),
        dma((z.n_kv - 1,)),
        dma((len(z.groups),)),
        dma((len(z.groups),)),
        dma((len(z.groups), rest)),
        dma((len(z.groups), rest)),
        dma((others,)),
        dma((others,)),
    ]


def spaces(*names):
    kinds = {"s": pltpu.SMEM, "v": pltpu.VMEM, "h": pl.ANY}
    return [pl.BlockSpec(memory_space=kinds[name]) for name in names]


def shards(
    queries, new_kv, kv_cache, kv_scales, context_lens, block_owner, block_index, out_weight
):
    n_kv, n_tp = lax.axis_size("kv"), lax.axis_size("tp")
    kv_heads = kv_cache.shape[3] // HD
    z = Sizes(n_kv, n_tp, kv_heads, kv_cache.shape[1], out_weight.shape[2])
    out = pl.pallas_call(
        functools.partial(layer, z),
        out_shape=jax.ShapeDtypeStruct((R, STEPS, z.cols), jnp.float32),
        in_specs=spaces(*"ssssvvhh"),
        out_specs=spaces("v")[0],
        scratch_shapes=scratch(z),
        compiler_params=pltpu.CompilerParams(
            vmem_limit_bytes=56 * 2**20, collective_id=0, has_side_effects=True
        ),
        name="layer",
    )(
        context_lens,
        block_owner,
        block_index,
        kv_scales.transpose(0, 2, 1),
        queries.transpose(1, 0, 2),
        new_kv.transpose(0, 2, 1, 3),
        kv_cache,
        out_weight,
    )
    return out.transpose(1, 0, 2).astype(jnp.bfloat16)


def solution(mesh):
    placed = (
        P(None, None, "tp"),
        P(None, None, None, "tp"),
        P(None, "kv", None, "tp"),
        P(None, "kv", "tp"),
        P(),
        P("kv"),
        P("kv"),
        P("tp", "kv", None),
    )
    return jax.shard_map(
        shards, mesh=mesh, in_specs=placed, out_specs=P(None, None, ("kv", "tp")), check_vma=False
    )
```

```python
import functools
import math

import jax
import jax.numpy as jnp
from jax import lax
from jax.experimental import pallas as pl
from jax.experimental.pallas import tpu as pltpu
from jax.sharding import PartitionSpec as P

HQ = 128
KVH = 8
HD = 128
R = 6
STEPS = 2
BLOCK = 256

very_negative = -1e30
MESH = pl.DeviceIdType.MESH


class Sizes:
    def __init__(self, n_kv, n_tp, kv_heads, slots, width):
        self.n_kv, self.n_tp, self.kv_heads, self.slots = n_kv, n_tp, kv_heads, slots
        self.share = HQ // KVH // n_kv
        self.used_rows = kv_heads * self.share * STEPS
        self.rows = -(-self.used_rows // 8) * 8
        self.all_rows = n_kv * self.rows
        self.depth = kv_heads * HD
        self.stack = R * self.rows
        self.message = self.stack + 8
        self.cols = width // (n_kv * n_tp)
        self.packed = self.cols % 256 == 0
        self.half = self.cols // 2 if self.packed else self.cols
        self.piece = 3 * self.half if self.packed else 2 * self.half
        self.width = width
        self.inner = self.share * HD
        self.pairs = n_kv // 2
        self.groups = [1] * n_tp
        self.load_parts = 4 if slots % 4 == 0 else 1


def flip(index, distance):
    result, bit = index, 1
    while bit <= distance:
        if distance & bit:
            result = result + bit * (1 - 2 * ((index // bit) % 2))
        bit *= 2
    return result


def row_head(z, shape):
    row = lax.broadcasted_iota(jnp.int32, shape, 0) % z.rows
    return row // (z.share * STEPS)


def by_head(z, head, pieces):
    result = pieces[-1]
    for k in range(z.kv_heads - 2, -1, -1):
        result = jnp.where(head == k, pieces[k], result)
    return result


def attend(
    z, lens, owner, number, scales, queries, msg, q_rows, kv_buf, qb, s_buf, m_buf, t_buf, n_buf, peak_buf, load, between, newest
):
    part = z.slots // z.load_parts
    head = row_head(z, (z.all_rows, HD))
    lane = lax.broadcasted_iota(jnp.int32, (z.all_rows, BLOCK), 1)
    factor = 1.0 / math.sqrt(HD)
    if z.used_rows < z.rows:
        q_rows[...] = jnp.zeros_like(q_rows)
    for r in range(R):
        flat = queries[r].astype(jnp.float32)
        for k in range(z.kv_heads):
            for j in range(z.n_kv):
                for g in range(z.share):
                    h = (k * z.n_kv + j) * z.share + g
                    row = (k * z.share + g) * STEPS
                    q_rows[r, j, row : row + STEPS, :] = flat[:, h * HD : (h + 1) * HD]
    for r in range(R):
        rows = q_rows[r].reshape(z.all_rows, HD)
        for k in range(z.kv_heads):
            qb[r, :, k * HD : (k + 1) * HD] = jnp.where(head == k, rows, 0.0).astype(jnp.bfloat16)
    blank = jnp.zeros((z.all_rows, HD), jnp.float32)
    m_buf[z.slots] = blank + very_negative
    t_buf[z.slots] = blank
    n_buf[z.slots] = blank

    def cap_of(b):
        own = owner[b]
        safe = jnp.minimum(own, R - 1)
        return safe, jnp.where(own < R, lens[safe], 0) - number[b] * BLOCK

    def score(b, before):
        safe, cap = cap_of(b)
        product = lax.dot_general(
            qb[safe], kv_buf[0, b], (((1,), (1,)), ((), ())), preferred_element_type=jnp.float32
        )
        scale = by_head(z, head, [jnp.full((z.all_rows, HD), scales[0, k, b] * factor) for k in range(z.kv_heads)])
        scale = jnp.concatenate([scale] * (BLOCK // HD), 1)
        masked = jnp.where(lane < cap, product * scale, very_negative)
        s_buf[b] = masked
        m_buf[b] = jnp.maximum(jnp.maximum(masked[:, :HD], masked[:, HD:]), m_buf[before])

    def mix(b, before):
        safe, cap = cap_of(b)
        top = peak_buf[safe]
        top = jnp.concatenate([top] * (BLOCK // HD), 1)
        weight = jnp.where(lane < cap, jnp.exp(s_buf[b] - top), 0.0)
        t_buf[b] = weight[:, :HD] + weight[:, HD:] + t_buf[before]
        product = jnp.dot(weight.astype(jnp.bfloat16), kv_buf[1, b], preferred_element_type=jnp.float32)
        mixed = by_head(z, head, [product[:, k * HD : (k + 1) * HD] * scales[1, k, b] for k in range(z.kv_heads)])
        n_buf[b] = mixed + n_buf[before]

    def sweep(which, step):
        def group(n, last):
            load(which, n).wait()
            last = list(last)
            for i in range(part):
                b = n * part + i
                own = owner[b]
                before = jnp.int32(z.slots)
                for r in range(R):
                    before = jnp.where(own == r, last[r], before)
                step(b, before)
                last = [jnp.where(own == r, b, last[r]) for r in range(R)]
            return tuple(last)

        return lax.fori_loop(0, z.load_parts, group, (jnp.int32(z.slots),) * R)

    fresh = newest()
    last = sweep(0, score)
    between()
    for r in range(R):
        peak_buf[r] = jnp.broadcast_to(m_buf[last[r]].max(1, keepdims=True), (z.all_rows, HD))
    last = sweep(1, mix)

    row = lax.broadcasted_iota(jnp.int32, (z.all_rows, HD), 0) % z.rows
    column = lax.broadcasted_iota(jnp.int32, (z.all_rows, HD), 1)
    peaks, totals = blank, blank
    for r in range(R):
        here = column == r * z.rows + row
        peaks = peaks + jnp.where(here, peak_buf[r], 0.0)
        totals = totals + jnp.where(here, t_buf[last[r]].sum(1, keepdims=True), 0.0)
        msg[:, r * z.rows : (r + 1) * z.rows, :] = n_buf[last[r]].reshape(z.n_kv, z.rows, HD)
    msg[:, z.stack :, :] = jnp.zeros((z.n_kv, 8, HD), jnp.float32)
    msg[:, z.stack : z.stack + 1, :] = peaks.reshape(z.n_kv, z.rows, HD).sum(1, keepdims=True)
    msg[:, z.stack + 1 : z.stack + 2, :] = totals.reshape(z.n_kv, z.rows, HD).sum(1, keepdims=True)
    return fresh


def layer(
    z, lens, owner, number, scales, queries, new_ref, cache, w_ref, out_ref,
    kv_buf, q_rows, qb, s_buf, m_buf, t_buf, n_buf, peak_buf, msg,
    w_buf, got, new_x, att, a_rows, sent1, got1, sent2, got2, sums, got3, whole,
    c_sem, w_sem, m_send, m_recv, send1, recv1, send2, recv2, send3, recv3,
):
    kv, tp = lax.axis_index("kv"), lax.axis_index("tp")
    high, side = kv // 2, kv % 2
    partner = kv + 1 - 2 * side
    order = list(range(z.pairs - 1, -1, -1))
    turns = [(e + 1) % z.n_tp for e in range(z.n_tp)]
    part = z.slots // z.load_parts

    def load(which, n):
        piece = pl.ds(n * part, part)
        return pltpu.make_async_copy(cache.at[which, piece], kv_buf.at[which, piece], c_sem.at[which, n])

    for which in range(2):
        for n in range(z.load_parts):
            load(which, n).start()

    barrier = pltpu.get_barrier_semaphore()
    for d in range(1, z.n_kv):
        pl.semaphore_signal(barrier, inc=1, device_id=(flip(kv, d), tp), device_id_type=MESH)
    for e in range(1, z.n_tp):
        pl.semaphore_signal(barrier, inc=1, device_id=(kv, (tp + e) % z.n_tp), device_id_type=MESH)

    block = z.inner // 4

    def load_weight(k, n):
        piece = pl.ds(n * block, block)
        return pltpu.make_async_copy(w_ref.at[k, piece], w_buf.at[k, piece], w_sem.at[k, n])

    def load_weights():
        for k in range(z.kv_heads):
            for n in range(4):
                load_weight(k, n).start()

    def newest():
        factor = 1.0 / math.sqrt(HD)
        newer = new_ref[...].astype(jnp.float32)
        small = row_head(z, (z.rows, HD))
        for a in range(2):
            for u in range(STEPS):
                for r in range(R):
                    pieces = [
                        jnp.broadcast_to(newer[a, r, u : u + 1, k * HD : (k + 1) * HD], (z.rows, HD))
                        for k in range(z.kv_heads)
                    ]
                    new_x[a, u, r * z.rows : (r + 1) * z.rows, :] = by_head(z, small, pieces)
        query = q_rows[:, kv].reshape(z.stack, HD)
        step_of = lax.broadcasted_iota(jnp.int32, (z.stack, 1), 0) % STEPS
        fresh = [(query * new_x[0, u]).sum(1, keepdims=True) * factor for u in range(STEPS)]
        fresh = [jnp.where(u <= step_of, fresh[u], very_negative) for u in range(STEPS)]
        fresh_top = functools.reduce(jnp.maximum, fresh)
        a_rows[...] = jnp.zeros_like(a_rows)
        return fresh, fresh_top, step_of

    fresh, fresh_top, step_of = attend(
        z, lens, owner, number, scales, queries, msg, q_rows, kv_buf, qb, s_buf, m_buf, t_buf, n_buf, peak_buf, load, load_weights, newest
    )
    pl.semaphore_wait(barrier, z.n_kv - 1 + z.n_tp - 1)

    def remote(src, dst, send, recv, target):
        return pltpu.make_async_remote_copy(
            src_ref=src, dst_ref=dst, send_sem=send, recv_sem=recv, device_id=target, device_id_type=MESH
        )

    exchange = []
    for d in range(z.n_kv - 1, 0, -1):
        there = flip(kv, d)
        copy = remote(msg.at[there], got.at[d - 1], m_send.at[d - 1], m_recv.at[d - 1], (there, tp))
        copy.start()
        exchange.append(copy)

    for copy in exchange:
        copy.wait_recv()
    spot = lax.broadcasted_iota(jnp.int32, (z.stack, HD), 0) == lax.broadcasted_iota(
        jnp.int32, (z.stack, HD), 1
    )

    def expand(values):
        return jnp.where(spot, values, 0.0).sum(1, keepdims=True)

    stats = [msg[kv, z.stack :, :]] + [got[d, z.stack :, :] for d in range(z.n_kv - 1)]
    peak = functools.reduce(jnp.maximum, [s[0:1] for s in stats])
    weights = [jnp.exp(s[0:1] - peak) for s in stats]
    total = functools.reduce(jnp.add, [w * s[1:2] for w, s in zip(weights, stats)])
    numer = expand(weights[0]) * msg[kv, : z.stack, :]
    for d in range(z.n_kv - 1):
        numer = numer + expand(weights[d + 1]) * got[d, : z.stack, :]
    peak, total = expand(peak), expand(total)
    top = jnp.maximum(peak, fresh_top)
    retain = jnp.exp(peak - top)
    fresh = [jnp.where(u <= step_of, jnp.exp(fresh[u] - top), 0.0) for u in range(STEPS)]
    numer, total = numer * retain, total * retain
    for u in range(STEPS):
        numer = numer + fresh[u] * new_x[1, u]
        total = total + fresh[u]
    att[...] = numer / total

    count = STEPS * R
    for c in range(z.kv_heads * z.share):
        for s in range(STEPS):
            a_rows[0, s * R : (s + 1) * R, c * HD : (c + 1) * HD] = att[
                pl.ds(c * STEPS + s, R, stride=z.rows), :
            ]
    a_rows[1, 0:8, :] = a_rows[0, 0:8, :]
    a_rows[1, 12 : 12 + count - 8, :] = a_rows[0, 8:count, :]
    low = a_rows[0].astype(jnp.bfloat16)
    late = a_rows[1].astype(jnp.bfloat16)

    for k in range(z.kv_heads):
        for n in range(4):
            load_weight(k, n).wait()

    def product(rows, start):
        columns = pl.ds(pl.multiple_of(start, z.half), z.half)
        parts = [
            jnp.dot(
                rows[:, k * z.inner : (k + 1) * z.inner],
                w_buf[k, :, columns],
                preferred_element_type=jnp.float32,
            )
            for k in range(z.kv_heads)
        ]
        return functools.reduce(jnp.add, parts)

    def fill(j, t, put):
        start = (j * z.n_tp + t) * z.cols
        first = product(low, start)
        if z.packed:
            second = product(late, start + z.half)
            put(slice(0, z.half), first[0:8])
            put(slice(z.half, 2 * z.half), second[0:8])
            put(slice(2 * z.half, 3 * z.half), first[8:16] + second[8:16])
        else:
            put(slice(0, z.half), first[0:8])
            put(slice(z.half, 2 * z.half), first[8:16])

    paired, spread, last, totals = [], [], [], []
    groups = z.groups
    firsts = [sum(groups[:i]) for i in range(len(groups))]

    def pair_step(i):
        for m in range(firsts[i], firsts[i] + groups[i]):
            for n, d in enumerate(order):

                def put(where, value):
                    sent1[m, n, :, where] = value

                fill(2 * flip(high, d) + 1 - side, (tp + turns[m]) % z.n_tp, put)
        piece = pl.ds(firsts[i], groups[i])
        copy = remote(sent1.at[piece], got1.at[piece], send1.at[i], recv1.at[i], (partner, tp))
        copy.start()
        paired.append(copy)

    def spread_step(i):
        paired[i].wait_recv()
        piece = pl.ds(firsts[i], groups[i])
        arriving = []
        for n, d in enumerate(order):
            there = 2 * flip(high, d) + side
            for m in range(firsts[i], firsts[i] + groups[i]):

                def put(where, value):
                    sent2[n, m, :, where] = value + got1[m, n, :, where]

                fill(there, (tp + turns[m]) % z.n_tp, put)
            if d > 0:
                copy = remote(
                    sent2.at[n, piece], got2.at[d - 1, piece], send2.at[i, d - 1], recv2.at[i, d - 1], (there, tp)
                )
                copy.start()
                arriving.append(copy)
        spread.append(arriving)

    def last_step(i):
        for copy in spread[i]:
            copy.wait_recv()
        for m in range(firsts[i], firsts[i] + groups[i]):
            e = turns[m]
            value = sent2[z.pairs - 1, m]
            for d in range(z.pairs - 1):
                value = value + got2[d, m]
            totals.append(value)
            if e > 0:
                sums[e - 1] = value
                there = (tp + e) % z.n_tp
                copy = remote(sums.at[e - 1], got3.at[e - 1], send3.at[e - 1], recv3.at[e - 1], (kv, there))
                copy.start()
                last.append(copy)

    ahead, lag = 2, 2
    for i in range(min(ahead, len(groups))):
        pair_step(i)
    for i in range(len(groups)):
        spread_step(i)
        if i + ahead < len(groups):
            pair_step(i + ahead)
        if i >= lag:
            last_step(i - lag)
    for i in range(max(len(groups) - lag, 0), len(groups)):
        last_step(i)
    value = totals[-1]
    for copy in last:
        copy.wait_recv()
    for e in range(z.n_tp - 1):
        value = value + got3[e]
    if z.packed:
        whole[0:8, : z.half] = value[:, : z.half]
        whole[0:8, z.half :] = value[:, z.half : 2 * z.half]
        whole[8:12, : z.half] = value[0:4, 2 * z.half :]
        whole[8:12, z.half :] = value[4:8, 2 * z.half :]
    else:
        whole[0:8, :] = value[:, : z.half]
        whole[8:16, :] = value[:, z.half :]
    for r in range(R):
        rows = [whole[s * R + r : s * R + r + 1, :] for s in range(STEPS)]
        out_ref[r] = jnp.concatenate(rows, 0).astype(jnp.bfloat16)
    for copy in exchange:
        copy.wait_send()
    for copy in paired + sum(spread, []) + last:
        copy.wait_send()


def scratch(z):
    f32, bf16 = jnp.float32, jnp.bfloat16
    dma = pltpu.SemaphoreType.DMA
    tile = (z.slots + 1, z.all_rows, HD)
    rest, others = max(z.pairs - 1, 1), max(z.n_tp - 1, 1)
    part = (8, z.piece)
    return [
        pltpu.VMEM((2, z.slots, BLOCK, z.depth), bf16),
        pltpu.VMEM((R, z.n_kv, z.rows, HD), f32),
        pltpu.VMEM((R, z.all_rows, z.depth), bf16),
        pltpu.VMEM((z.slots, z.all_rows, BLOCK), f32),
        pltpu.VMEM(tile, f32),
        pltpu.VMEM(tile, f32),
        pltpu.VMEM(tile, f32),
        pltpu.VMEM((R, z.all_rows, HD), f32),
        pltpu.VMEM((z.n_kv, z.message, HD), f32),
        pltpu.VMEM((z.kv_heads, z.inner, z.width), bf16),
        pltpu.VMEM((z.n_kv - 1, z.message, HD), f32),
        pltpu.VMEM((2, STEPS, z.stack, HD), f32),
        pltpu.VMEM((z.stack, HD), f32),
        pltpu.VMEM((2, 16, z.kv_heads * z.inner), f32),
        pltpu.VMEM((z.n_tp, z.pairs, *part), f32),
        pltpu.VMEM((z.n_tp, z.pairs, *part), f32),
        pltpu.VMEM((z.pairs, z.n_tp, *part), f32),
        pltpu.VMEM((rest, z.n_tp, *part), f32),
        pltpu.VMEM((others, *part), f32),
        pltpu.VMEM((others, *part), f32),
        pltpu.VMEM((16, z.cols), f32),
        dma((2, z.load_parts)),
        dma((z.kv_heads, 4)),
        dma((z.n_kv - 1,)),
        dma((z.n_kv - 1,)),
        dma((len(z.groups),)),
        dma((len(z.groups),)),
        dma((len(z.groups), rest)),
        dma((len(z.groups), rest)),
        dma((others,)),
        dma((others,)),
    ]


def spaces(*names):
    kinds = {"s": pltpu.SMEM, "v": pltpu.VMEM, "h": pl.ANY}
    return [pl.BlockSpec(memory_space=kinds[name]) for name in names]


def shards(
    queries, new_kv, kv_cache, kv_scales, context_lens, block_owner, block_index, out_weight
):
    n_kv, n_tp = lax.axis_size("kv"), lax.axis_size("tp")
    kv_heads = kv_cache.shape[3] // HD
    z = Sizes(n_kv, n_tp, kv_heads, kv_cache.shape[1], out_weight.shape[2])
    out = pl.pallas_call(
        functools.partial(layer, z),
        out_shape=jax.ShapeDtypeStruct((R, STEPS, z.cols), jnp.bfloat16),
        in_specs=spaces(*"ssssvvhh"),
        out_specs=spaces("v")[0],
        scratch_shapes=scratch(z),
        compiler_params=pltpu.CompilerParams(
            vmem_limit_bytes=56 * 2**20, collective_id=0, has_side_effects=True
        ),
        name="layer",
    )(
        context_lens,
        block_owner,
        block_index,
        kv_scales.transpose(0, 2, 1),
        queries.transpose(1, 0, 2),
        new_kv.transpose(0, 2, 1, 3),
        kv_cache,
        out_weight,
    )
    return out.transpose(1, 0, 2)


def solution(mesh):
    placed = (
        P(None, None, "tp"),
        P(None, None, None, "tp"),
        P(None, "kv", None, "tp"),
        P(None, "kv", "tp"),
        P(),
        P("kv"),
        P("kv"),
        P("tp", "kv", None),
    )
    return jax.shard_map(
        shards, mesh=mesh, in_specs=placed, out_specs=P(None, None, ("kv", "tp")), check_vma=False
    )
```
